1024 devices in a mesh: grp: 64 (over z, y), loc: 16 (over x, core).
Axes of the slice: x: 8, y: 8, z: 8, core: 2. Of those that a mesh axis runs over, the one named last changes fastest.
Arguments:
- out_grad: bfloat16 [8192, 7168], P(('grp', 'loc')), may hold values from -6 to 6
- route_prob: bfloat16 [8192, 4, 2], P(('grp', 'loc')), may hold values from 0.019897461 to 1
- group_ids: int32 [8192, 4], P(('grp', 'loc')), may hold values from 0 to 63, as said below
- gate_pre: bfloat16 [64, 512, 2048], P('grp', None, 'loc'), may hold values from -6 to 6
- down_weight: bfloat16 [131072, 7168], P(('grp', 'loc')), may hold values from -0.0625 to 0.0625
Outputs:
- pre_grad: bfloat16 [64, 512, 2048], P('grp', None, 'loc')
- route_grad: float32 [8192, 4, 2], P(('grp', 'loc'))
The draws below stay inside these ranges and needn't reach their ends.
Inputs may be any that keep to these rules, and one draw needn't show every extreme that they name: `group_ids`: for device (g, l) and its row s = t * 4 + k, the group is (g + p_l(s mod 64)) mod 64, with one permutation p_l of the groups for each index l of loc; so a token's 4 groups differ, every row of every group is filled exactly once, and a device names one group at most 1 times.
All inputs are finite; a program needn't handle non-finite values.
Results may differ from the reference program's by a relative error of at most 0.0012.
Values may be sent and summed in bfloat16 or wider, within the bound.
No kernel may reach another device: no remote copies, remote signals or barrier semaphores. Data moves between devices by JAX's collectives and lax.ppermute only.
A program may use at most 32 MiB of HBM per device.

```python
import math
import jax
import jax.numpy as jnp
from jax import lax

D = 7168
FF = 1024
EXP_GRP = 2
GTOP = 4
TOK_DEV = 8
TOKENS = 8192
EXPERTS = 128
ROWS_GRP = 512
N_GRP = 64
N_LOC = 16


def draw_group_ids(key, part):
    key = jax.random.fold_in(key, 11)
    lane_keys = jax.random.split(key, N_LOC)
    orders = jax.vmap(lambda one_key: jax.random.permutation(one_key, N_GRP))(lane_keys).astype(jnp.int32)
    residue = jnp.arange(TOK_DEV * GTOP, dtype=jnp.int32) % N_GRP
    offsets = orders[:, residue]
    groups = jnp.arange(N_GRP, dtype=jnp.int32)
    chosen = (groups[:, None, None] + offsets[None, :, :]) % N_GRP
    return chosen.reshape(TOKENS, GTOP).astype(jnp.int32)


def shard_levels(key, shape, cuts, low, high):
    loudness, own = 1.0, jax.random.fold_in(key, 6)
    for position, shards_of in cuts:
        draws = jnp.exp(jax.random.uniform(jax.random.fold_in(own, position), (shards_of,), jnp.float32, low / len(cuts), high / len(cuts)))
        loudness = loudness * jnp.repeat(draws, shape[position] // shards_of).reshape([-1 if axis == position else 1 for axis in range(len(shape))])
    return loudness


def normal_values(key, extent, width, reach, pieces=(), kind=jnp.bfloat16):
    drawn = width * jax.random.normal(key, extent, jnp.float32)
    if pieces:
        drawn = drawn * shard_levels(key, extent, pieces, -0.22, 0.18)
    return jnp.clip(drawn, -reach, reach).astype(kind)


def setup_inputs(seed: int = 0) -> dict:
    seeds = jax.random.split(jax.random.key(seed), 6)
    out_grad = normal_values(seeds[0], (TOKENS, D), 1.0, 6.0, ((0, 1024),))
    route_prob = jnp.clip(jnp.exp(math.log(1.0) - 3.9171631 * jax.random.uniform(seeds[1], (TOKENS, GTOP, EXP_GRP), jnp.float32) ** shard_levels(seeds[1], (TOKENS, GTOP, EXP_GRP), ((0, 1024),), -0.2, 0.2)), 0.019897461, 1.0).astype(jnp.bfloat16)
    group_ids = draw_group_ids(jax.random.fold_in(seeds[5], 71), 0)
    gate_pre = normal_values(seeds[3], (N_GRP, ROWS_GRP, EXP_GRP * FF), 1.5, 6.0, ((0, 64), (2, 16)))
    down_weight = normal_values(seeds[4], (EXPERTS * FF, D), D ** -0.5, 0.0625, ((0, 1024),))
    return {"out_grad": out_grad, "route_prob": route_prob, "group_ids": group_ids, "gate_pre": gate_pre, "down_weight": down_weight}


def reference(out_grad, route_prob, group_ids, gate_pre, down_weight):
    rows_lane = TOK_DEV * GTOP
    grp_table = group_ids.reshape(N_GRP, N_LOC, rows_lane).astype(jnp.int32)
    lane_index = jnp.broadcast_to(jnp.arange(N_LOC, dtype=jnp.int32)[None, :, None], grp_table.shape)
    row_index = jnp.broadcast_to(jnp.arange(rows_lane, dtype=jnp.int32)[None, None, :], grp_table.shape)
    grad_rows = jnp.repeat(out_grad.reshape(N_GRP, N_LOC, TOK_DEV, D), GTOP, axis=2)
    prob_rows = route_prob.reshape(N_GRP, N_LOC, rows_lane, EXP_GRP)
    routed_grad = jnp.zeros((N_GRP, N_LOC, rows_lane, D), jnp.bfloat16)
    routed_grad = routed_grad.at[grp_table, lane_index, row_index].set(grad_rows).reshape(N_GRP, ROWS_GRP, D)
    routed_prob = jnp.zeros((N_GRP, N_LOC, rows_lane, EXP_GRP), jnp.bfloat16)
    routed_prob = routed_prob.at[grp_table, lane_index, row_index].set(prob_rows).reshape(N_GRP, ROWS_GRP, EXP_GRP)
    weights = down_weight.reshape(N_GRP, EXP_GRP * FF, D)

    def per_group(items):
        grad_group, prob_group, gate_group, weight_group = items
        hidden_grad = jnp.dot(grad_group, weight_group.T, preferred_element_type=jnp.float32)
        gate_value = gate_group.astype(jnp.float32)
        sigma = jax.nn.sigmoid(gate_value)
        active = gate_value * sigma
        slope = sigma * (1.0 + gate_value * (1.0 - sigma))
        scale = jnp.repeat(prob_group.astype(jnp.float32), FF, axis=1)
        grad_out = (scale * hidden_grad * slope).astype(jnp.bfloat16)
        prob_grad = jnp.sum((active * hidden_grad).reshape(ROWS_GRP, EXP_GRP, FF), axis=2)
        return grad_out, prob_grad

    pre_grad, prob_grad = lax.map(per_group, (routed_grad, routed_prob, gate_pre, weights))
    prob_grad = prob_grad.reshape(N_GRP, N_LOC, rows_lane, EXP_GRP)
    route_grad = prob_grad[grp_table, lane_index, row_index].reshape(TOKENS, GTOP, EXP_GRP)
    return pre_grad, route_grad
```

```python
import functools

import jax
import jax.numpy as jnp
from jax import lax
from jax.experimental import pallas as pl
from jax.experimental.pallas import tpu as pltpu
from jax.sharding import PartitionSpec as P

SUB = 8
LANES = 128
SHARES = (7,)
NT = (((1,), (1,)), ((), ()))
TN = (((0,), (0,)), ((), ()))
BF = jnp.bfloat16
F32 = jnp.float32


def iota(shape, dim):
    return lax.broadcasted_iota(jnp.int32, shape, dim)


def chunks(model):
    unit, found, first = model // sum(SHARES), [], 0
    for share in SHARES:
        found.append((first, unit * share // SUB))
        first += unit * share
    return found


def send_kernel(grad_ref, gid_ref, prob_ref, *out_refs):
    tok = grad_ref.shape[0]
    rows = out_refs[0].shape[0]
    shape = (rows, SUB * tok)
    row, col = iota(shape, 0), iota(shape, 1)
    same_sub = (row % SUB) == (col // tok)
    slot = row // SUB
    pick = jnp.zeros(shape, F32)
    prob = jnp.zeros((rows, prob_ref.shape[1]), F32)
    for k in range(gid_ref.shape[0]):
        here = jnp.where(same_sub & (slot == gid_ref[k : k + 1, :]), 1.0, 0.0)
        pick += here
        prob += lax.dot_general(here.astype(BF), prob_ref[k], NT, preferred_element_type=F32)
    for out_ref, (first, wide) in zip(out_refs, chunks(grad_ref.shape[1])):
        starts = [first + e * wide for e in range(SUB)]
        grad = jnp.concatenate([grad_ref[:, at : at + wide] for at in starts], axis=0)
        out_ref[:, :wide] = jnp.dot(pick.astype(BF), grad, preferred_element_type=F32).astype(BF)
    out_refs[-1][:, wide:] = prob.astype(BF)


def pick_kernel(recv_ref, source_ref, *refs):
    out_ref = refs[-1]
    rows = source_ref.shape[0]
    wide = out_ref.shape[1]
    lane_rows = rows // SUB
    pick = jnp.where(iota((rows, recv_ref.shape[0]), 1) == source_ref[...], 1.0, 0.0).astype(BF)
    out_ref[:rows, :] = jnp.dot(pick, recv_ref[:, :wide], preferred_element_type=F32).astype(BF)
    if out_ref.shape[0] == rows:
        return
    prob = jnp.dot(pick[:lane_rows], recv_ref[:, wide:], preferred_element_type=F32)
    prob = jnp.transpose(prob)[:SUB]
    pad = jnp.zeros((SUB, wide - lane_rows), F32)
    out_ref[rows:, :] = jnp.concatenate([prob, pad], axis=1).astype(BF)


def terms_kernel(place_ref, *refs):
    parts, (own_w, mate_w, own_gate, mate_gate, pre_ref, give_ref, sum_ref) = refs[:-7], refs[-7:]
    count = len(parts) // len(SHARES)
    shards = parts[-count:]
    rows = (shards[0].shape[0] - SUB) // SUB
    width = own_w.shape[0]
    hidden = jnp.zeros((count * rows, 2 * width), F32)
    for c, (first, wide) in enumerate(chunks(own_w.shape[1])):
        here = parts[c * count : (c + 1) * count]
        for e in range(SUB):
            left = jnp.concatenate([ref[e * rows : (e + 1) * rows, :] for ref in here], axis=0)
            cols = slice(first + e * wide, first + (e + 1) * wide)
            right = jnp.concatenate([own_w[:, cols], mate_w[:, cols]], axis=0)
            hidden += lax.dot_general(left, right, NT, preferred_element_type=F32)
    expert = jnp.where(iota((SUB, width), 0) == place_ref[count], 1.0, 0.0).astype(BF)
    terms = []
    for i, ref in enumerate(shards):
        at = pl.ds(pl.multiple_of(place_ref[i] * rows, rows), rows)
        scale = lax.dot_general(
            ref[SUB * rows :, :rows], expert, TN, preferred_element_type=F32
        )
        total = jnp.zeros((rows, width), F32)
        for half, gate in enumerate((own_gate, mate_gate)):
            grad = hidden[i * rows : (i + 1) * rows, half * width : (half + 1) * width]
            value = gate[at, :].astype(F32)
            sigma = jax.nn.sigmoid(value)
            slope = sigma * (1.0 + value * (1.0 - sigma))
            total += value * sigma * grad
            result = (scale * grad * slope).astype(BF)
            if half == 0:
                pre_ref[at, :] = result
            else:
                give_ref[i * rows : (i + 1) * rows, :] = result
        terms.append(total)
    sums = lax.dot_general(
        jnp.ones((SUB, width), F32),
        jnp.concatenate(terms, axis=0),
        NT,
        precision=lax.Precision.HIGHEST,
        preferred_element_type=F32,
    )
    sum_ref[...] = jnp.zeros(sum_ref.shape, F32)
    for i in range(count):
        sum_ref[pl.ds(place_ref[i], 1), 0, :rows] = sums[:1, i * rows : (i + 1) * rows]


def join_kernel(place_ref, half_ref, got_ref, out_ref):
    rows = got_ref.shape[0] // place_ref.shape[0]
    out_ref[...] = half_ref[...]
    for i in range(place_ref.shape[0]):
        at = pl.ds(pl.multiple_of(place_ref[i] * rows, rows), rows)
        out_ref[at, :] = got_ref[i * rows : (i + 1) * rows, :]


VMEM = pl.BlockSpec(memory_space=pltpu.VMEM)
SMEM = pl.BlockSpec(memory_space=pltpu.SMEM)
ANY = pl.BlockSpec(memory_space=pl.ANY)
PARAMS = pltpu.CompilerParams(vmem_limit_bytes=48 * 1024 * 1024)


def call(kernel, specs, shapes, *args):
    single = not isinstance(shapes, list)
    return pl.pallas_call(
        kernel,
        in_specs=specs,
        out_specs=VMEM if single else [VMEM] * len(shapes),
        out_shape=shapes,
        compiler_params=PARAMS,
    )(*args)


def shape(dims, kind):
    return jax.ShapeDtypeStruct(dims, kind)


def body(out_grad, route_prob, group_ids, gate_pre, down_weight):
    tok, model = out_grad.shape
    top = group_ids.shape[1]
    experts = route_prob.shape[2]
    groups = lax.axis_size("grp")
    locs = lax.axis_size("loc")
    chips = locs // 2
    rows = tok * top
    gate_rows = gate_pre[0]
    width = gate_rows.shape[1]
    my_group = lax.axis_index("grp")
    loc = lax.axis_index("loc")
    swap = [(l, l ^ 1) for l in range(locs)]
    ahead = [(l, (l + (2 if l % 2 == 0 else -2)) % locs) for l in range(locs)]

    gid = jnp.tile(group_ids.T, (1, SUB))
    prob = jnp.pad(
        jnp.transpose(route_prob, (1, 2, 0)), ((0, 0), (0, LANES - experts), (0, 0))
    )
    prob = jnp.tile(prob, (1, 1, SUB))
    plan = chunks(model)
    extra = [LANES if c == len(plan) - 1 else 0 for c in range(len(plan))]
    sends = call(
        send_kernel,
        [VMEM] * 3,
        [shape((groups * SUB, wide + more), BF) for (_, wide), more in zip(plan, extra)],
        out_grad,
        gid,
        prob,
    )
    move = functools.partial(lax.ppermute, axis_name="loc")
    recvs = [
        lax.all_to_all(
            send.reshape(groups, SUB, -1), "grp", split_axis=0, concat_axis=0, tiled=True
        ).reshape(groups * SUB, -1)
        for send in sends
    ]
    mate_w = move(down_weight, perm=swap)
    mate_gate = move(gate_rows, perm=swap)
    flat = group_ids.reshape(rows)
    source = (2 * my_group - flat) % groups
    source = (source[None, :] * SUB + jnp.arange(SUB, dtype=jnp.int32)[:, None]).reshape(-1, 1)
    nears, fars = [], []
    for c, (_, wide) in enumerate(plan):
        early = (mate_w, mate_gate) if c == 0 else ()
        own = call(
            pick_kernel,
            [VMEM] * 2 + [ANY] * len(early),
            shape((SUB * rows + (SUB if extra[c] else 0), wide), BF),
            recvs[c],
            source,
            *early,
        )
        nears.append([own])
        fars.append([move(own, perm=swap)])
    for step in range(chips // 2):
        for near, far in zip(nears, fars):
            near.append(move(near[-1], perm=ahead))
            if step < chips // 2 - 1:
                far.append(move(far[-1], perm=ahead))
    shards = [one for near, far in zip(nears, fars) for one in near + far[1:]]
    count = len(shards) // len(plan)

    def places(at):
        chip, core = at // 2, at % 2
        step = 2 * core - 1
        hops = [(k, core) for k in range(chips // 2 + 1)] + [(k, 1 - core) for k in range(1, chips // 2)]
        return jnp.stack([(chip + step * k) % chips * 2 + c for k, c in hops]).astype(jnp.int32)

    place = jnp.concatenate([places(loc), (loc // (locs // experts)).reshape(1)])
    half, give, sums = call(
        terms_kernel,
        [SMEM] + [VMEM] * (len(shards) + 4),
        [
            shape(gate_rows.shape, BF),
            shape((count * rows, width), BF),
            shape((locs, 1, LANES), F32),
        ],
        place,
        *shards,
        down_weight,
        mate_w,
        gate_rows,
        mate_gate,
    )
    got = move(give, perm=swap)
    parts = lax.all_to_all(sums, "loc", split_axis=0, concat_axis=0, tiled=True)
    lane = jnp.sum(parts.reshape(experts, locs // experts, LANES), axis=1)
    lane = jnp.pad(lane[:, :rows].reshape(experts * rows), (0, LANES - experts * rows))
    back = lax.all_to_all(
        jnp.broadcast_to(lane, (groups, 1, LANES)), "grp", split_axis=0, concat_axis=0, tiled=True
    )[:, 0]
    pre = call(join_kernel, [SMEM, VMEM, VMEM], shape(gate_rows.shape, BF), places(loc ^ 1), half, got)
    wanted = jnp.tile(flat, experts)[None, :] == jnp.arange(groups, dtype=jnp.int32)[:, None]
    route = jnp.sum(jnp.where(wanted, back[:, : experts * rows], 0.0), axis=0)
    route = jnp.transpose(route.reshape(experts, tok, top), (1, 2, 0))
    return pre[None], route


def solution(mesh):
    placed = (
        P(("grp", "loc"), None),
        P(("grp", "loc"), None, None),
        P(("grp", "loc"), None),
        P("grp", None, "loc"),
        P(("grp", "loc"), None),
    )
    return jax.shard_map(
        body,
        mesh=mesh,
        in_specs=placed,
        out_specs=(P("grp", None, "loc"), P(("grp", "loc"), None, None)),
        check_vma=False,
    )
```

```python
import functools

import jax
import jax.numpy as jnp
from jax import lax
from jax.experimental import pallas as pl
from jax.experimental.pallas import tpu as pltpu
from jax.sharding import PartitionSpec as P

SUB = 8
LANES = 128
NT = (((1,), (1,)), ((), ()))
TN = (((0,), (0,)), ((), ()))
BF = jnp.bfloat16
F32 = jnp.float32


def iota(shape, dim):
    return lax.broadcasted_iota(jnp.int32, shape, dim)


def send_kernel(grad_ref, gid_ref, prob_ref, out_ref):
    tok = grad_ref.shape[0]
    rows = out_ref.shape[0]
    wide = grad_ref.shape[1] // SUB
    slot = iota((rows, tok), 0) // SUB
    pick = jnp.zeros((rows, tok), F32)
    prob = jnp.zeros((rows, prob_ref.shape[1]), F32)
    for k in range(gid_ref.shape[0]):
        here = jnp.where(slot == gid_ref[k : k + 1, :], 1.0, 0.0)
        pick += here
        prob += lax.dot_general(here.astype(BF), prob_ref[k], NT, preferred_element_type=F32)
    dims = (tok, SUB * tok)
    spread = jnp.where(iota(dims, 1) % tok == iota(dims, 0), 1.0, 0.0).astype(BF)
    pick = jnp.dot(pick.astype(BF), spread, preferred_element_type=F32)
    dims = pick.shape
    pick = jnp.where(iota(dims, 0) % SUB == iota(dims, 1) // tok, pick, 0.0)
    dims = (prob.shape[1], LANES)
    spread = jnp.where(iota(dims, 0) == iota(dims, 1), 1.0, 0.0).astype(BF)
    prob = jnp.dot(prob.astype(BF), spread, preferred_element_type=F32)
    grad = jnp.concatenate([grad_ref[:, e * wide : (e + 1) * wide] for e in range(SUB)], axis=0)
    out_ref[:, :wide] = jnp.dot(pick.astype(BF), grad, preferred_element_type=F32).astype(BF)
    out_ref[:, wide:] = prob.astype(BF)


def pick_kernel(group_ref, recv_ref, gid_ref, *refs):
    out_ref = refs[-1]
    top, tok = gid_ref.shape
    lane_rows = top * tok
    rows = SUB * lane_rows
    wide = out_ref.shape[1]
    slots = recv_ref.shape[0]
    dims = (rows, tok)
    spread = jnp.where(iota(dims, 0) % lane_rows // top == iota(dims, 1), 1.0, 0.0).astype(BF)
    gids = lax.dot_general(
        spread, gid_ref[...].astype(F32).astype(BF), NT, preferred_element_type=F32
    )
    dims = (rows, top)
    gids = jnp.sum(jnp.where(iota(dims, 0) % top == iota(dims, 1), gids, 0.0), axis=1, keepdims=True)
    source = 2 * group_ref[0] - gids.astype(jnp.int32)
    groups = slots // SUB
    source = jnp.where(source < 0, source + groups, source)
    source = jnp.where(source >= groups, source - groups, source)
    source = source * SUB + iota((rows, 1), 0) // lane_rows
    pick = jnp.where(iota((rows, slots), 1) == source, 1.0, 0.0).astype(BF)
    out_ref[:rows, :] = jnp.dot(pick, recv_ref[:, :wide], preferred_element_type=F32).astype(BF)
    prob = jnp.dot(pick[:lane_rows], recv_ref[:, wide:], preferred_element_type=F32)
    prob = jnp.transpose(prob)[:SUB]
    pad = jnp.zeros((SUB, wide - lane_rows), F32)
    out_ref[rows:, :] = jnp.concatenate([prob, pad], axis=1).astype(BF)


def terms_kernel(place_ref, *refs):
    shards, last_prob = refs[:-8], refs[-8]
    own_w, mate_w, own_gate, mate_gate, pre_ref, give_ref, sum_ref = refs[-7:]
    count = len(shards)
    rows = (shards[0].shape[0] - SUB) // SUB
    width, model = own_w.shape
    wide = model // SUB
    hidden = jnp.zeros((count * rows, 2 * width), F32)
    for e in range(SUB):
        left = jnp.concatenate([ref[e * rows : (e + 1) * rows, :] for ref in shards], axis=0)
        cols = slice(e * wide, (e + 1) * wide)
        right = jnp.concatenate([own_w[:, cols], mate_w[:, cols]], axis=0)
        hidden += lax.dot_general(left, right, NT, preferred_element_type=F32)
    expert = jnp.where(iota((SUB, width), 0) == place_ref[count], 1.0, 0.0).astype(BF)
    terms = []
    for i, ref in enumerate(shards):
        at = pl.ds(pl.multiple_of(place_ref[i] * rows, rows), rows)
        prob = last_prob[...] if i == count - 1 else ref[SUB * rows :, :]
        scale = lax.dot_general(
            prob[:, :rows], expert, TN, preferred_element_type=F32
        )
        total = jnp.zeros((rows, width), F32)
        for half, gate in enumerate((own_gate, mate_gate)):
            grad = hidden[i * rows : (i + 1) * rows, half * width : (half + 1) * width]
            value = gate[at, :].astype(F32)
            sigma = jax.nn.sigmoid(value)
            slope = sigma * (1.0 + value * (1.0 - sigma))
            total += value * sigma * grad
            result = (scale * grad * slope).astype(BF)
            if half == 0:
                pre_ref[at, :] = result
            else:
                give_ref[i * rows : (i + 1) * rows, :] = result
        terms.append(total)
    sums = lax.dot_general(
        jnp.ones((SUB, width), F32),
        jnp.concatenate(terms, axis=0),
        NT,
        precision=lax.Precision.HIGHEST,
        preferred_element_type=F32,
    )
    sum_ref[...] = jnp.zeros(sum_ref.shape, F32)
    for i in range(count):
        sum_ref[pl.ds(place_ref[i], 1), 0, :rows] = sums[:1, i * rows : (i + 1) * rows]


def prob_kernel(shard_ref, out_ref):
    out_ref[...] = shard_ref[shard_ref.shape[0] - SUB :, :]


def join_kernel(place_ref, half_ref, got_ref, out_ref):
    rows = got_ref.shape[0] // place_ref.shape[0]
    out_ref[...] = half_ref[...]
    for i in range(place_ref.shape[0]):
        at = pl.ds(pl.multiple_of(place_ref[i] * rows, rows), rows)
        out_ref[at, :] = got_ref[i * rows : (i + 1) * rows, :]


BLOCK = pl.BlockSpec()
VMEM = pl.BlockSpec(memory_space=pltpu.VMEM)
SMEM = pl.BlockSpec(memory_space=pltpu.SMEM)
ANY = pl.BlockSpec(memory_space=pl.ANY)
PARAMS = pltpu.CompilerParams(vmem_limit_bytes=12 * 1024 * 1024)


def hbm(*arrays):
    return [pltpu.with_memory_space_constraint(one, pltpu.HBM) for one in arrays]


def call(kernel, specs, shapes, *args):
    return pl.pallas_call(
        kernel, in_specs=specs, out_shape=shapes, compiler_params=PARAMS
    )(*args)


def shape(dims, kind):
    return jax.ShapeDtypeStruct(dims, kind)


def body(out_grad, route_prob, group_ids, gate_pre, down_weight):
    tok, model = out_grad.shape
    top = group_ids.shape[1]
    experts = route_prob.shape[2]
    groups = lax.axis_size("grp")
    locs = lax.axis_size("loc")
    chips = locs // 2
    rows = tok * top
    gate_rows = gate_pre[0]
    width = gate_rows.shape[1]
    my_group = lax.axis_index("grp")
    loc = lax.axis_index("loc")
    swap = [(l, l ^ 1) for l in range(locs)]
    ahead = [(l, (l + (2 if l % 2 == 0 else -2)) % locs) for l in range(locs)]

    gid = group_ids.T
    prob = jnp.transpose(route_prob, (1, 2, 0))
    wide = model // SUB
    send = call(
        send_kernel, [BLOCK] * 3, shape((groups * SUB, wide + LANES), BF), *hbm(out_grad, gid, prob)
    )
    move = functools.partial(lax.ppermute, axis_name="loc")
    recv = lax.all_to_all(
        send.reshape(groups, SUB, -1), "grp", split_axis=0, concat_axis=0, tiled=True
    ).reshape(groups * SUB, -1)
    mate_w = move(down_weight, perm=swap)
    mate_gate = move(gate_rows, perm=swap)
    own = call(
        pick_kernel,
        [SMEM, BLOCK, BLOCK, ANY, ANY],
        shape((SUB * rows + SUB, wide), BF),
        my_group.reshape(1),
        recv,
        gid,
        mate_w,
        mate_gate,
    )
    near, far = [own], [move(own, perm=swap)]
    for step in range(chips // 2):
        near.append(move(near[-1], perm=ahead))
        if step < chips // 2 - 1:
            far.append(move(far[-1], perm=ahead))
    shards = near + far[1:]
    count = len(shards)

    def places(at):
        chip, core = at // 2, at % 2
        step = 2 * core - 1
        hops = [(k, core) for k in range(chips // 2 + 1)] + [(k, 1 - core) for k in range(1, chips // 2)]
        return jnp.stack([(chip + step * k) % chips * 2 + c for k, c in hops]).astype(jnp.int32)

    place = jnp.concatenate([places(loc), (loc // (locs // experts)).reshape(1)])
    last_prob = call(prob_kernel, [VMEM], shape((SUB, wide), BF), far[-1])
    half, give, sums = call(
        terms_kernel,
        [SMEM] + [VMEM] * (count + 5),
        [
            shape(gate_rows.shape, BF),
            shape((count * rows, width), BF),
            shape((locs, 1, LANES), F32),
        ],
        place,
        *shards,
        last_prob,
        down_weight,
        mate_w,
        gate_rows,
        mate_gate,
    )
    got = move(give, perm=swap)
    parts = lax.all_to_all(sums, "loc", split_axis=0, concat_axis=0, tiled=True)
    lane = jnp.sum(parts.reshape(experts, locs // experts, LANES), axis=1)
    lane = jnp.pad(lane[:, :rows].reshape(experts * rows), (0, LANES - experts * rows))
    back = lax.all_to_all(
        jnp.broadcast_to(lane, (groups, 1, LANES)), "grp", split_axis=0, concat_axis=0, tiled=True
    )[:, 0]
    pre = call(join_kernel, [SMEM, BLOCK, BLOCK], shape(gate_rows.shape, BF), places(loc ^ 1), *hbm(half), got)
    flat = group_ids.reshape(rows)
    wanted = jnp.tile(flat, experts)[None, :] == jnp.arange(groups, dtype=jnp.int32)[:, None]
    route = jnp.sum(jnp.where(wanted, back[:, : experts * rows], 0.0), axis=0)
    route = jnp.transpose(route.reshape(experts, tok, top), (1, 2, 0))
    return pre[None], route


def solution(mesh):
    placed = (
        P(("grp", "loc"), None),
        P(("grp", "loc"), None, None),
        P(("grp", "loc"), None),
        P("grp", None, "loc"),
        P(("grp", "loc"), None),
    )
    return jax.shard_map(
        body,
        mesh=mesh,
        in_specs=placed,
        out_specs=(P("grp", None, "loc"), P(("grp", "loc"), None, None)),
        check_vma=False,
    )
```

```python
import functools

import jax
import jax.numpy as jnp
from jax import lax
from jax.experimental import pallas as pl
from jax.experimental.pallas import tpu as pltpu
from jax.sharding import PartitionSpec as P

SUB = 8
LANES = 128
NT = (((1,), (1,)), ((), ()))
TN = (((0,), (0,)), ((), ()))
BF = jnp.bfloat16
F32 = jnp.float32


def iota(shape, dim):
    return lax.broadcasted_iota(jnp.int32, shape, dim)


def send_kernel(grad_ref, gid_ref, prob_ref, out_ref):
    tok = grad_ref.shape[0]
    rows = out_ref.shape[0]
    wide = grad_ref.shape[1] // SUB
    slot = iota((rows, tok), 0) // SUB
    pick = jnp.zeros((rows, tok), F32)
    prob = jnp.zeros((rows, prob_ref.shape[1]), F32)
    for k in range(gid_ref.shape[0]):
        here = jnp.where(slot == gid_ref[k : k + 1, :], 1.0, 0.0)
        pick += here
        prob += lax.dot_general(here.astype(BF), prob_ref[k], NT, preferred_element_type=F32)
    dims = (tok, SUB * tok)
    spread = jnp.where(iota(dims, 1) % tok == iota(dims, 0), 1.0, 0.0).astype(BF)
    pick = jnp.dot(pick.astype(BF), spread, preferred_element_type=F32)
    dims = pick.shape
    pick = jnp.where(iota(dims, 0) % SUB == iota(dims, 1) // tok, pick, 0.0)
    dims = (prob.shape[1], LANES)
    spread = jnp.where(iota(dims, 0) == iota(dims, 1), 1.0, 0.0).astype(BF)
    prob = jnp.dot(prob.astype(BF), spread, preferred_element_type=F32)
    grad = jnp.concatenate([grad_ref[:, e * wide : (e + 1) * wide] for e in range(SUB)], axis=0)
    out_ref[:, :wide] = jnp.dot(pick.astype(BF), grad, preferred_element_type=F32).astype(BF)
    out_ref[:, wide:] = prob.astype(BF)


def pick_kernel(group_ref, recv_ref, gid_ref, *refs):
    out_ref = refs[-1]
    top, tok = gid_ref.shape
    lane_rows = top * tok
    rows = SUB * lane_rows
    wide = out_ref.shape[1]
    slots = recv_ref.shape[0]
    dims = (rows, tok)
    spread = jnp.where(iota(dims, 0) % lane_rows // top == iota(dims, 1), 1.0, 0.0).astype(BF)
    gids = lax.dot_general(
        spread, gid_ref[...].astype(F32).astype(BF), NT, preferred_element_type=F32
    )
    dims = (rows, top)
    gids = jnp.sum(jnp.where(iota(dims, 0) % top == iota(dims, 1), gids, 0.0), axis=1, keepdims=True)
    source = 2 * group_ref[0] - gids.astype(jnp.int32)
    groups = slots // SUB
    source = jnp.where(source < 0, source + groups, source)
    source = jnp.where(source >= groups, source - groups, source)
    source = source * SUB + iota((rows, 1), 0) // lane_rows
    pick = jnp.where(iota((rows, slots), 1) == source, 1.0, 0.0).astype(BF)
    out_ref[:rows, :] = jnp.dot(pick, recv_ref[:, :wide], preferred_element_type=F32).astype(BF)
    prob = jnp.dot(pick[:lane_rows], recv_ref[:, wide:], preferred_element_type=F32)
    prob = jnp.transpose(prob)[:SUB]
    pad = jnp.zeros((SUB, wide - lane_rows), F32)
    out_ref[rows:, :] = jnp.concatenate([prob, pad], axis=1).astype(BF)


def multiply(shards, own_w, mate_w):
    rows = (shards[0].shape[0] - SUB) // SUB
    width, model = own_w.shape
    wide = model // SUB
    hidden = jnp.zeros((len(shards) * rows, 2 * width), F32)
    for e in range(SUB):
        left = jnp.concatenate([ref[e * rows : (e + 1) * rows, :] for ref in shards], axis=0)
        cols = slice(e * wide, (e + 1) * wide)
        right = jnp.concatenate([own_w[:, cols], mate_w[:, cols]], axis=0)
        hidden += lax.dot_general(left, right, NT, preferred_element_type=F32)
    return hidden


def finish(place_ref, first, shards, hidden, gates, pre_ref, give_ref, sum_ref):
    rows = (shards[0].shape[0] - SUB) // SUB
    width = gates[0].shape[1]
    mine = place_ref[place_ref.shape[0] - 1]
    expert = jnp.where(iota((SUB, width), 0) == mine, 1.0, 0.0).astype(BF)
    terms = []
    for i, ref in enumerate(shards):
        at = pl.ds(pl.multiple_of(place_ref[first + i] * rows, rows), rows)
        scale = lax.dot_general(
            ref[SUB * rows :, :rows], expert, TN, preferred_element_type=F32
        )
        total = jnp.zeros((rows, width), F32)
        for half, gate in enumerate(gates):
            grad = hidden[i * rows : (i + 1) * rows, half * width : (half + 1) * width]
            value = gate[at, :].astype(F32)
            sigma = jax.nn.sigmoid(value)
            slope = sigma * (1.0 + value * (1.0 - sigma))
            total += value * sigma * grad
            result = (scale * grad * slope).astype(BF)
            if half == 0:
                pre_ref[at, :] = result
            else:
                give_ref[(first + i) * rows : (first + i + 1) * rows, :] = result
        terms.append(total)
    sums = lax.dot_general(
        jnp.ones((SUB, width), F32),
        jnp.concatenate(terms, axis=0),
        NT,
        precision=lax.Precision.HIGHEST,
        preferred_element_type=F32,
    )
    for i in range(len(shards)):
        sum_ref[pl.ds(place_ref[first + i], 1), 0, :rows] = sums[:1, i * rows : (i + 1) * rows]


def early_kernel(place_ref, *refs):
    shards, (own_w, mate_w, own_gate, mate_gate, pre_ref, give_ref, sum_ref) = refs[:-7], refs[-7:]
    hidden = multiply(shards, own_w, mate_w)
    pre_ref[...] = jnp.zeros(pre_ref.shape, BF)
    give_ref[...] = jnp.zeros(give_ref.shape, BF)
    sum_ref[...] = jnp.zeros(sum_ref.shape, F32)
    gates = (own_gate, mate_gate)
    finish(place_ref, 0, shards, hidden, gates, pre_ref, give_ref, sum_ref)


def last_kernel(place_ref, shard, own_w, mate_w, own_gate, mate_gate, *refs):
    ins, outs = refs[:3], refs[3:]
    hidden = multiply([shard], own_w, mate_w)
    for source, target in zip(ins, outs):
        target[...] = source[...]
    finish(place_ref, place_ref.shape[0] - 2, [shard], hidden, (own_gate, mate_gate), *outs)


def join_kernel(place_ref, half_ref, got_ref, out_ref):
    rows = got_ref.shape[0] // place_ref.shape[0]
    out_ref[...] = half_ref[...]
    for i in range(place_ref.shape[0]):
        at = pl.ds(pl.multiple_of(place_ref[i] * rows, rows), rows)
        out_ref[at, :] = got_ref[i * rows : (i + 1) * rows, :]


BLOCK = pl.BlockSpec()
VMEM = pl.BlockSpec(memory_space=pltpu.VMEM)
SMEM = pl.BlockSpec(memory_space=pltpu.SMEM)
ANY = pl.BlockSpec(memory_space=pl.ANY)
PARAMS = pltpu.CompilerParams(vmem_limit_bytes=12 * 1024 * 1024)


def hbm(*arrays):
    return [pltpu.with_memory_space_constraint(one, pltpu.HBM) for one in arrays]


def call(kernel, specs, shapes, *args):
    return pl.pallas_call(
        kernel, in_specs=specs, out_shape=shapes, compiler_params=PARAMS
    )(*args)


def shape(dims, kind):
    return jax.ShapeDtypeStruct(dims, kind)


def body(out_grad, route_prob, group_ids, gate_pre, down_weight):
    tok, model = out_grad.shape
    top = group_ids.shape[1]
    experts = route_prob.shape[2]
    groups = lax.axis_size("grp")
    locs = lax.axis_size("loc")
    chips = locs // 2
    rows = tok * top
    gate_rows = gate_pre[0]
    width = gate_rows.shape[1]
    my_group = lax.axis_index("grp")
    loc = lax.axis_index("loc")
    swap = [(l, l ^ 1) for l in range(locs)]
    ahead = [(l, (l + (2 if l % 2 == 0 else -2)) % locs) for l in range(locs)]

    gid = group_ids.T
    prob = jnp.transpose(route_prob, (1, 2, 0))
    wide = model // SUB
    send = call(
        send_kernel, [BLOCK] * 3, shape((groups * SUB, wide + LANES), BF), *hbm(out_grad, gid, prob)
    )
    move = functools.partial(lax.ppermute, axis_name="loc")
    recv = lax.all_to_all(
        send.reshape(groups, SUB, -1), "grp", split_axis=0, concat_axis=0, tiled=True
    ).reshape(groups * SUB, -1)
    mate_w = move(down_weight, perm=swap)
    mate_gate = move(gate_rows, perm=swap)
    own = call(
        pick_kernel,
        [SMEM, BLOCK, BLOCK, ANY, ANY],
        shape((SUB * rows + SUB, wide), BF),
        my_group.reshape(1),
        recv,
        gid,
        mate_w,
        mate_gate,
    )
    near, far = [own], [move(own, perm=swap)]
    for step in range(chips // 2):
        near.append(move(near[-1], perm=ahead))
        if step < chips // 2 - 1:
            far.append(move(far[-1], perm=ahead))
    shards = near[:-1] + far[1:] + near[-1:]
    count = len(shards)

    def places(at):
        chip, core = at // 2, at % 2
        step = 2 * core - 1
        last = chips // 2
        hops = [(k, core) for k in range(last)] + [(k, 1 - core) for k in range(1, last)]
        hops.append((last, core))
        return jnp.stack([(chip + step * k) % chips * 2 + c for k, c in hops]).astype(jnp.int32)

    place = jnp.concatenate([places(loc), (loc // (locs // experts)).reshape(1)])
    results = [
        shape(gate_rows.shape, BF),
        shape((count * rows, width), BF),
        shape((locs, 1, LANES), F32),
    ]
    shared = (down_weight, mate_w, gate_rows, mate_gate)
    early = call(
        early_kernel, [SMEM] + [VMEM] * (count + 3), results, place, *shards[:-1], *shared
    )
    half, give, sums = call(
        last_kernel, [SMEM] + [VMEM] * 8, results, place, shards[-1], *shared, *early
    )
    got = move(give, perm=swap)
    parts = lax.all_to_all(sums, "loc", split_axis=0, concat_axis=0, tiled=True)
    lane = jnp.sum(parts.reshape(experts, locs // experts, LANES), axis=1)
    lane = jnp.pad(lane[:, :rows].reshape(experts * rows), (0, LANES - experts * rows))
    back = lax.all_to_all(
        jnp.broadcast_to(lane, (groups, 1, LANES)), "grp", split_axis=0, concat_axis=0, tiled=True
    )[:, 0]
    pre = call(join_kernel, [SMEM, BLOCK, BLOCK], shape(gate_rows.shape, BF), places(loc ^ 1), *hbm(half), got)
    flat = group_ids.reshape(rows)
    wanted = jnp.tile(flat, experts)[None, :] == jnp.arange(groups, dtype=jnp.int32)[:, None]
    route = jnp.sum(jnp.where(wanted, back[:, : experts * rows], 0.0), axis=0)
    route = jnp.transpose(route.reshape(experts, tok, top), (1, 2, 0))
    return pre[None], route


def solution(mesh):
    placed = (
        P(("grp", "loc"), None),
        P(("grp", "loc"), None, None),
        P(("grp", "loc"), None),
        P("grp", None, "loc"),
        P(("grp", "loc"), None),
    )
    return jax.shard_map(
        body,
        mesh=mesh,
        in_specs=placed,
        out_specs=(P("grp", None, "loc"), P(("grp", "loc"), None, None)),
        check_vma=False,
    )
```
